128 devices in a mesh: dp: 128 (over y, z, x, core).
Axes of the slice: x: 4, y: 4, z: 4, core: 2. Of those that a mesh axis runs over, the one named last changes fastest.
Arguments:
- images: bfloat16 [32768, 1152], P('dp'), may hold values from -0.7 to 0.7
- texts: bfloat16 [32768, 1152], P('dp'), may hold values from -0.9 to 0.9
- partner: int32 [3, 128], replicated, may hold values from 0 to 127, as said below
- logit_scale: float32 [1], replicated, may hold values from 4 to 16
- logit_bias: float32 [1], replicated, may hold values from -3 to -1
Outputs:
- image_grad: float32 [32768, 1152], P('dp')
- text_grad: float32 [32768, 1152], P('dp')
- row_loss: float32 [32768], P('dp')
The draws below stay inside these ranges and needn't reach their ends.
Inputs may be any that keep to these rules, and one draw needn't show every extreme that they name: partner[r, d] = d XOR m_r, with m_r of 1 to 127 for round r, the 3 numbers distinct.
All inputs are finite; a program needn't handle non-finite values.
Results may differ from the reference program's by a relative error of at most 0.0023.
Values may be sent and summed in bfloat16 or wider, within the bound.
No kernel may reach another device: no remote copies, remote signals or barrier semaphores. Data moves between devices by JAX's collectives and lax.ppermute only.
A program may use at most 64 MiB of HBM per device.

```python
import math
import jax
import jax.numpy as jnp
from jax import lax

D = 1152
B = 256
ROUNDS = 3
NB = 128
TOKENS = 32768


cluster_count = 16


def shared_parts(key):
    cluster_ids = jax.random.randint(jax.random.fold_in(key, 101), (TOKENS,), 0, cluster_count).astype(jnp.int32)
    base_level = jax.random.uniform(jax.random.fold_in(key, 102), (TOKENS, D), jnp.float32, 0.0001, 1.0 - 0.0001)
    center_level = jax.random.uniform(jax.random.fold_in(key, 103), (cluster_count // 2, D), jnp.float32, 0.0001, 1.0 - 0.0001)
    return (cluster_ids, base_level, center_level)


def as_normal(level):
    return 1.4142135 * lax.erf_inv(2.0 * level - 1.0)


def cluster_rows(cluster_ids, centers):
    cluster_sign = (1 - 2 * (cluster_ids % 2)).astype(jnp.float32)
    return centers[cluster_ids // 2] * cluster_sign[:, None]


def draw_images(key, part):
    cluster_ids, base_level, center_level = shared_parts(key)
    key = jax.random.fold_in(key, 7)
    scale_level = jax.random.uniform(key, (TOKENS, 1), jnp.float32, 0.0, 1.0)
    base = as_normal(base_level)
    centers = as_normal(center_level)
    row_scale = 0.3 * jnp.power(10.0, scale_level)
    center_part = cluster_rows(cluster_ids, centers)
    values = (0.8 * base + 1.2 * center_part) * row_scale * D ** (-0.5)
    return jnp.clip(values, -0.7, 0.7).astype(jnp.bfloat16)


def draw_texts(key, part):
    cluster_ids, base_level, center_level = shared_parts(key)
    key = jax.random.fold_in(key, 9)
    noise_level = jax.random.uniform(jax.random.fold_in(key, 1), (TOKENS, D), jnp.float32, 0.0001, 1.0 - 0.0001)
    scale_level = jax.random.uniform(jax.random.fold_in(key, 2), (TOKENS, 1), jnp.float32, 0.0, 1.0)
    base = as_normal(base_level)
    centers = as_normal(center_level)
    noise = as_normal(noise_level)
    row_scale = 0.3 * jnp.power(10.0, scale_level)
    center_part = cluster_rows(cluster_ids, centers)
    values = (0.8 * base + 1.1 * center_part + 0.7 * noise) * row_scale * D ** (-0.5)
    return jnp.clip(values, -0.9, 0.9).astype(jnp.bfloat16)


def draw_partner(key, part):
    key = jax.random.fold_in(key, 5)
    picks = jax.random.permutation(key, NB - 1)[:ROUNDS] + 1
    blocks = jnp.arange(NB, dtype=jnp.int32)
    return jnp.bitwise_xor(blocks[None, :], picks[:, None].astype(jnp.int32)).astype(jnp.int32)


def setup_inputs(seed: int = 0) -> dict:
    arg_keys = jax.random.split(jax.random.key(seed), 6)
    images = draw_images(jax.random.fold_in(arg_keys[5], 71), 0)
    texts = draw_texts(jax.random.fold_in(arg_keys[5], 71), 0)
    partner = draw_partner(jax.random.fold_in(arg_keys[5], 71), 0)
    logit_scale = jnp.clip(jnp.exp(jax.random.uniform(arg_keys[3], (1,), jnp.float32, math.log(4.0), math.log(16.0))), 4.0, 16.0)
    logit_bias = jnp.clip(jax.random.uniform(arg_keys[4], (1,), jnp.float32, -3.0, -1.0), -3.0, -1.0)
    return dict(images=images, texts=texts, partner=partner, logit_scale=logit_scale, logit_bias=logit_bias)


NORM_EPS = 1e-06

def unit_rows(embedding):
    values = embedding.astype(jnp.float32)
    length = jnp.sqrt(lax.optimization_barrier(jnp.sum(values * values, axis=-1, keepdims=True)) + NORM_EPS)
    return (values / length, length)

def through_half(values):
    rounded = lax.optimization_barrier(values.astype(jnp.bfloat16))
    return rounded.astype(jnp.float32)

def finish(unit_value, length, summed):
    radial = lax.optimization_barrier(jnp.sum(unit_value * summed, axis=-1, keepdims=True))
    return (summed - unit_value * radial) / length

def reference(images, texts, partner, logit_scale, logit_bias):
    img_unit, img_length = unit_rows(images)
    txt_unit, txt_length = unit_rows(texts)
    img_blocks = through_half(img_unit).reshape(NB, B, D)
    txt_blocks = through_half(txt_unit).reshape(NB, B, D)
    scale_value = logit_scale[0]
    bias_value = logit_bias[0]
    identity = jnp.eye(B, dtype=jnp.float32)
    own_blocks = jnp.arange(NB, dtype=jnp.int32)
    img_sum = jnp.zeros((NB, B, D), jnp.float32)
    txt_sum = jnp.zeros((NB, B, D), jnp.float32)
    row_total = jnp.zeros((NB, B), jnp.float32)
    for column_set in range(ROUNDS + 1):
        if column_set == 0:
            columns = own_blocks
            positive = identity
        else:
            columns = partner[column_set - 1].astype(jnp.int32)
            positive = jnp.zeros_like(identity)

        def one_block(block_pair):
            img_rows, column_id = block_pair
            txt_cols = txt_blocks[column_id]
            logits = scale_value * jnp.dot(img_rows, txt_cols.T, preferred_element_type=jnp.float32, precision=lax.Precision.HIGHEST) + bias_value
            row_part = lax.optimization_barrier(jnp.sum(jax.nn.softplus((1.0 - 2.0 * positive) * logits), axis=-1))
            weights = through_half(jax.nn.sigmoid(logits) - positive)
            img_part = scale_value * jnp.dot(weights, txt_cols, preferred_element_type=jnp.float32, precision=lax.Precision.HIGHEST)
            term_part = scale_value * jnp.dot(weights.T, img_rows, preferred_element_type=jnp.float32, precision=lax.Precision.HIGHEST)
            return (row_part, img_part, term_part)
        row_part, img_part, term_part = lax.map(one_block, (img_blocks, columns))
        row_total = row_total + row_part
        img_sum = img_sum + img_part
        if column_set == 0:
            txt_sum = txt_sum + term_part
        else:
            txt_sum = txt_sum.at[columns].add(through_half(term_part))
    image_grad = finish(img_unit, img_length, img_sum.reshape(TOKENS, D))
    text_grad = finish(txt_unit, txt_length, txt_sum.reshape(TOKENS, D))
    row_loss = row_total.reshape(TOKENS) / ((ROUNDS + 1) * B)
    return (image_grad, text_grad, row_loss)
```

```python
import functools

import jax
import jax.numpy as jnp
from jax import lax
from jax.experimental import pallas as pl
from jax.experimental.pallas import tpu as pltpu
from jax.sharding import PartitionSpec as P

ROUNDS = 3
NORM_EPS = 1e-06
PIECE = 8
VMEM_BYTES = 48 * 1024 * 1024
NT = (((1,), (1,)), ((), ()))


def inverse_length(values):
    return lax.rsqrt(jnp.sum(values * values, axis=-1, keepdims=True) + NORM_EPS)


def halve_kernel(images_ref, texts_ref, half_ref):
    for slot, source in enumerate((images_ref, texts_ref)):
        values = source[...].astype(jnp.float32)
        half_ref[slot] = (values * inverse_length(values)).astype(jnp.bfloat16)


def halve(images, texts):
    rows, width = images.shape
    step = rows // 4
    return pl.pallas_call(
        halve_kernel,
        grid=(rows // step,),
        in_specs=[pl.BlockSpec((step, width), lambda i: (i, 0))] * 2,
        out_specs=pl.BlockSpec((2, step, width), lambda i: (0, i, 0)),
        out_shape=jax.ShapeDtypeStruct((2, rows, width), jnp.bfloat16),
        compiler_params=pltpu.CompilerParams(vmem_limit_bytes=VMEM_BYTES),
    )(images, texts)


def own_kernel(scalars_ref, half_ref, img_sum_ref, txt_sum_ref, row_ref):
    scale, bias = scalars_ref[0], scalars_ref[1]
    img, txt = half_ref[0], half_ref[1]
    rows = img.shape[0]
    diagonal = lax.broadcasted_iota(jnp.int32, (rows, rows), 0) == lax.broadcasted_iota(
        jnp.int32, (rows, rows), 1
    )
    logits = scale * lax.dot_general(img, txt, NT, preferred_element_type=jnp.float32) + bias
    signed = jnp.where(diagonal, -logits, logits)
    row_ref[...] = jnp.sum(softplus(signed), axis=-1, keepdims=True)
    positive = jnp.where(diagonal, 1.0, 0.0)
    weights = (sigmoid(logits) - positive).astype(jnp.bfloat16)
    img_sum_ref[...] = scale * jnp.dot(weights, txt, preferred_element_type=jnp.float32)
    turned = scale * lax.dot_general(txt, img, NT, preferred_element_type=jnp.float32) + bias
    weights = (sigmoid(turned) - positive).astype(jnp.bfloat16)
    txt_sum_ref[...] = scale * jnp.dot(weights, img, preferred_element_type=jnp.float32)


def softplus(x):
    return jnp.maximum(x, 0.0) + jnp.log1p(jnp.exp(-jnp.abs(x)))


def sigmoid(x):
    return 1.0 / (1.0 + jnp.exp(-x))


def own_terms(scalars, half):
    _, rows, width = half.shape
    return pl.pallas_call(
        own_kernel,
        in_specs=[
            pl.BlockSpec(memory_space=pltpu.SMEM),
            pl.BlockSpec(memory_space=pltpu.VMEM),
        ],
        out_specs=[pl.BlockSpec(memory_space=pltpu.VMEM)] * 3,
        out_shape=[
            jax.ShapeDtypeStruct((rows, width), jnp.float32),
            jax.ShapeDtypeStruct((rows, width), jnp.float32),
            jax.ShapeDtypeStruct((rows, 1), jnp.float32),
        ],
        compiler_params=pltpu.CompilerParams(vmem_limit_bytes=VMEM_BYTES),
        cost_estimate=pl.CostEstimate(
            flops=8 * rows * rows * width, bytes_accessed=12 * rows * width, transcendentals=4 * rows * rows
        ),
    )(scalars, half)


def route_kernel(flips_ref, same_ref, other_ref, out_ref):
    chips = same_ref.shape[0]
    for r in range(ROUNDS):
        chip_flip = flips_ref[r] // 2
        core_flip = flips_ref[r] % 2
        for core, source in enumerate((same_ref, other_ref)):

            @pl.when(core_flip == core)
            def _():
                def copy(t, carry):
                    out_ref[t, r] = source[lax.bitwise_xor(t, chip_flip)]
                    return carry

                lax.fori_loop(0, chips, copy, 0, unroll=8)


def route(flips, same, other):
    chips, piece, width = same.shape
    return pl.pallas_call(
        route_kernel,
        in_specs=[pl.BlockSpec(memory_space=pltpu.SMEM)]
        + [pl.BlockSpec(memory_space=pltpu.VMEM)] * 2,
        out_specs=pl.BlockSpec(memory_space=pltpu.VMEM),
        out_shape=jax.ShapeDtypeStruct((chips, ROUNDS, piece, width), same.dtype),
        compiler_params=pltpu.CompilerParams(vmem_limit_bytes=VMEM_BYTES),
    )(flips, same, other)


def finish(values, summed):
    inverse = inverse_length(values)
    unit = values * inverse
    radial = jnp.sum(unit * summed, axis=-1, keepdims=True)
    return (summed - unit * radial) * inverse


def rounds_kernel(
    scalars_ref, images_ref, texts_ref, half_ref, far_ref, img_sum_ref, txt_sum_ref, row_ref,
    image_grad_ref, text_grad_ref, loss_ref,
):
    scale, bias = scalars_ref[0], scalars_ref[1]
    img, txt = half_ref[0], half_ref[1]
    rows, width = img.shape
    pieces = far_ref.shape[0] // 2
    row_total = row_ref[...]
    img_sum = img_sum_ref[...]
    txt_sum = txt_sum_ref[...]
    for r in range(ROUNDS):
        far_img = far_ref[:pieces, r].reshape(rows, width)
        far_txt = far_ref[pieces:, r].reshape(rows, width)
        logits = scale * lax.dot_general(img, far_txt, NT, preferred_element_type=jnp.float32) + bias
        row_total = row_total + jnp.sum(softplus(logits), axis=-1, keepdims=True)
        weights = sigmoid(logits).astype(jnp.bfloat16)
        img_sum = img_sum + scale * jnp.dot(weights, far_txt, preferred_element_type=jnp.float32)
        turned = scale * lax.dot_general(txt, far_img, NT, preferred_element_type=jnp.float32) + bias
        weights = sigmoid(turned).astype(jnp.bfloat16)
        term = scale * jnp.dot(weights, far_img, preferred_element_type=jnp.float32)
        txt_sum = txt_sum + term.astype(jnp.bfloat16).astype(jnp.float32)
    image_grad_ref[...] = finish(images_ref[...].astype(jnp.float32), img_sum)
    text_grad_ref[...] = finish(texts_ref[...].astype(jnp.float32), txt_sum)
    loss_ref[...] = row_total * (1.0 / ((ROUNDS + 1) * rows))


def all_rounds(scalars, images, texts, half, far, img_sum, txt_sum, row_total):
    rows, width = images.shape
    return pl.pallas_call(
        rounds_kernel,
        in_specs=[pl.BlockSpec(memory_space=pltpu.SMEM)]
        + [pl.BlockSpec(memory_space=pltpu.VMEM)] * 7,
        out_specs=[pl.BlockSpec(memory_space=pltpu.VMEM)] * 3,
        out_shape=[
            jax.ShapeDtypeStruct((rows, width), jnp.float32),
            jax.ShapeDtypeStruct((rows, width), jnp.float32),
            jax.ShapeDtypeStruct((rows, 1), jnp.float32),
        ],
        compiler_params=pltpu.CompilerParams(vmem_limit_bytes=VMEM_BYTES),
    )(scalars, images, texts, half, far, img_sum, txt_sum, row_total)


def body(num_dev, images, texts, partner, logit_scale, logit_bias):
    rows, width = images.shape
    chips = num_dev // 2
    same_core = [[2 * chip + core for chip in range(chips)] for core in range(2)]
    exchange = functools.partial(
        lax.all_to_all, axis_name="dp", split_axis=0, concat_axis=0, tiled=True, axis_index_groups=same_core
    )
    scalars = jnp.concatenate([logit_scale, logit_bias])
    flips = partner[:, 0]
    half = halve(images, texts)
    spread = exchange(half.reshape(chips, PIECE, width))
    img_sum, txt_sum, row_total = own_terms(scalars, half)
    sibling = lax.ppermute(spread, "dp", [(i, i ^ 1) for i in range(num_dev)])
    far = exchange(route(flips, spread, sibling))
    image_grad, text_grad, loss = all_rounds(
        scalars, images, texts, half, far, img_sum, txt_sum, row_total
    )
    return image_grad, text_grad, loss.reshape(rows)


def solution(mesh):
    return jax.shard_map(
        functools.partial(body, mesh.devices.size),
        mesh=mesh,
        in_specs=(P("dp", None), P("dp", None), P(), P(), P()),
        out_specs=(P("dp", None), P("dp", None), P("dp")),
        check_vma=False,
    )
```

```python
import functools

import jax
import jax.numpy as jnp
from jax import lax
from jax.experimental import pallas as pl
from jax.experimental.pallas import tpu as pltpu
from jax.sharding import PartitionSpec as P

ROUNDS = 3
NORM_EPS = 1e-06
PIECE = 8
VMEM_BYTES = 20 * 1024 * 1024
FULL_VMEM_BYTES = 61 * 1024 * 1024
NT = (((1,), (1,)), ((), ()))


def inverse_length(values):
    return lax.rsqrt(jnp.sum(values * values, axis=-1, keepdims=True) + NORM_EPS)


def halve_kernel(images_ref, texts_ref, half_ref):
    for slot, source in enumerate((images_ref, texts_ref)):
        values = source[...].astype(jnp.float32)
        half_ref[slot] = (values * inverse_length(values)).astype(jnp.bfloat16)


def halve(images, texts):
    rows, width = images.shape
    step = rows // 2
    return pl.pallas_call(
        halve_kernel,
        grid=(rows // step,),
        in_specs=[pl.BlockSpec((step, width), lambda i: (i, 0))] * 2,
        out_specs=pl.BlockSpec((2, step, width), lambda i: (0, i, 0)),
        out_shape=jax.ShapeDtypeStruct((2, rows, width), jnp.bfloat16),
        compiler_params=pltpu.CompilerParams(vmem_limit_bytes=FULL_VMEM_BYTES),
    )(images, texts)


def own_kernel(scalars_ref, half_ref, img_sum_ref, txt_sum_ref, loss_ref):
    scale, bias = scalars_ref[0], scalars_ref[1]
    img, txt = half_ref[0], half_ref[1]
    rows = img.shape[0]
    diagonal = lax.broadcasted_iota(jnp.int32, (rows, rows), 0) == lax.broadcasted_iota(
        jnp.int32, (rows, rows), 1
    )
    logits = scale * lax.dot_general(img, txt, NT, preferred_element_type=jnp.float32) + bias
    signed = jnp.where(diagonal, -logits, logits)
    loss_ref[...] = softplus(signed)
    positive = jnp.where(diagonal, 1.0, 0.0)
    weights = (sigmoid(logits) - positive).astype(jnp.bfloat16)
    img_sum_ref[...] = scale * jnp.dot(weights, txt, preferred_element_type=jnp.float32)
    turned = scale * lax.dot_general(txt, img, NT, preferred_element_type=jnp.float32) + bias
    weights = (sigmoid(turned) - positive).astype(jnp.bfloat16)
    txt_sum_ref[...] = scale * jnp.dot(weights, img, preferred_element_type=jnp.float32)


def softplus(x):
    return jnp.maximum(x, 0.0) + jnp.log1p(jnp.exp(-jnp.abs(x)))


def sigmoid(x):
    return 1.0 / (1.0 + jnp.exp(-x))


def own_terms(scalars, half):
    _, rows, width = half.shape
    return pl.pallas_call(
        own_kernel,
        in_specs=[
            pl.BlockSpec(memory_space=pltpu.SMEM),
            pl.BlockSpec(memory_space=pltpu.VMEM),
        ],
        out_specs=[pl.BlockSpec(memory_space=pltpu.VMEM)] * 3,
        out_shape=[
            jax.ShapeDtypeStruct((rows, width), jnp.float32),
            jax.ShapeDtypeStruct((rows, width), jnp.float32),
            jax.ShapeDtypeStruct((rows, rows), jnp.float32),
        ],
        compiler_params=pltpu.CompilerParams(vmem_limit_bytes=VMEM_BYTES),
        cost_estimate=pl.CostEstimate(
            flops=8 * rows * rows * width, bytes_accessed=12 * rows * width, transcendentals=4 * rows * rows
        ),
    )(scalars, half)


def route_kernel(flips_ref, same_ref, other_ref, out_ref):
    chips = same_ref.shape[0]
    for r in range(ROUNDS):
        chip_flip = flips_ref[r] // 2
        core_flip = flips_ref[r] % 2
        for core, source in enumerate((same_ref, other_ref)):

            @pl.when(core_flip == core)
            def _():
                def copy(t, carry):
                    out_ref[t, r] = source[lax.bitwise_xor(t, chip_flip)]
                    return carry

                lax.fori_loop(0, chips, copy, 0, unroll=8)


def route(flips, same, other):
    chips, piece, width = same.shape
    return pl.pallas_call(
        route_kernel,
        in_specs=[pl.BlockSpec(memory_space=pltpu.SMEM)]
        + [pl.BlockSpec(memory_space=pltpu.VMEM)] * 2,
        out_specs=pl.BlockSpec(memory_space=pltpu.VMEM),
        out_shape=jax.ShapeDtypeStruct((chips, ROUNDS, piece, width), same.dtype),
        compiler_params=pltpu.CompilerParams(vmem_limit_bytes=VMEM_BYTES),
    )(flips, same, other)


def finish(values, summed):
    inverse = inverse_length(values)
    unit = values * inverse
    radial = jnp.sum(unit * summed, axis=-1, keepdims=True)
    return (summed - unit * radial) * inverse


def rounds_kernel(
    scalars_ref, images_ref, texts_ref, half_ref, far_ref, img_sum_ref, txt_sum_ref, own_loss_ref,
    image_grad_ref, text_grad_ref, loss_ref,
):
    scale, bias = scalars_ref[0], scalars_ref[1]
    img, txt = half_ref[0], half_ref[1]
    rows, width = img.shape
    pieces = far_ref.shape[0] // 2
    losses = own_loss_ref[...]
    img_sum = img_sum_ref[...]
    txt_sum = txt_sum_ref[...]
    for r in range(ROUNDS):
        far_img = far_ref[:pieces, r].reshape(rows, width)
        far_txt = far_ref[pieces:, r].reshape(rows, width)
        logits = scale * lax.dot_general(img, far_txt, NT, preferred_element_type=jnp.float32) + bias
        losses = losses + softplus(logits)
        weights = sigmoid(logits).astype(jnp.bfloat16)
        img_sum = img_sum + scale * jnp.dot(weights, far_txt, preferred_element_type=jnp.float32)
        turned = scale * lax.dot_general(txt, far_img, NT, preferred_element_type=jnp.float32) + bias
        weights = sigmoid(turned).astype(jnp.bfloat16)
        term = scale * jnp.dot(weights, far_img, preferred_element_type=jnp.float32)
        txt_sum = txt_sum + term.astype(jnp.bfloat16).astype(jnp.float32)
    image_grad_ref[...] = finish(images_ref[...].astype(jnp.float32), img_sum)
    text_grad_ref[...] = finish(texts_ref[...].astype(jnp.float32), txt_sum)
    loss_ref[...] = jnp.sum(losses.T, axis=0, keepdims=True) * (1.0 / ((ROUNDS + 1) * rows))


def all_rounds(scalars, images, texts, half, far, img_sum, txt_sum, losses):
    rows, width = images.shape
    return pl.pallas_call(
        rounds_kernel,
        in_specs=[pl.BlockSpec(memory_space=pltpu.SMEM)]
        + [pl.BlockSpec(memory_space=pltpu.VMEM)] * 7,
        out_specs=[pl.BlockSpec(memory_space=pltpu.VMEM)] * 3,
        out_shape=[
            jax.ShapeDtypeStruct((rows, width), jnp.float32),
            jax.ShapeDtypeStruct((rows, width), jnp.float32),
            jax.ShapeDtypeStruct((1, rows), jnp.float32),
        ],
        compiler_params=pltpu.CompilerParams(vmem_limit_bytes=VMEM_BYTES),
    )(scalars, images, texts, half, far, img_sum, txt_sum, losses)


def body(num_dev, images, texts, partner, logit_scale, logit_bias):
    rows, width = images.shape
    chips = num_dev // 2
    same_core = [[2 * chip + core for chip in range(chips)] for core in range(2)]
    exchange = functools.partial(
        lax.all_to_all, axis_name="dp", split_axis=0, concat_axis=0, tiled=True, axis_index_groups=same_core
    )
    scalars = jnp.concatenate([logit_scale, logit_bias])
    flips = partner[:, 0]
    half = halve(images, texts)
    spread = exchange(half.reshape(chips, PIECE, width))
    half, spread = lax.optimization_barrier((half, spread))
    sibling = lax.ppermute(spread, "dp", [(i, i ^ 1) for i in range(num_dev)])
    img_sum, txt_sum, losses = own_terms(scalars, half)
    sibling, img_sum = lax.optimization_barrier((sibling, img_sum))
    far = exchange(route(flips, spread, sibling))
    image_grad, text_grad, loss = all_rounds(
        scalars, images, texts, half, far, img_sum, txt_sum, losses
    )
    return image_grad, text_grad, loss.reshape(rows)


def solution(mesh):
    return jax.shard_map(
        functools.partial(body, mesh.devices.size),
        mesh=mesh,
        in_specs=(P("dp", None), P("dp", None), P(), P(), P()),
        out_specs=(P("dp", None), P("dp", None), P("dp")),
        check_vma=False,
    )
```

```python
import functools

import jax
import jax.numpy as jnp
from jax import lax
from jax.experimental import pallas as pl
from jax.experimental.pallas import tpu as pltpu
from jax.sharding import PartitionSpec as P

ROUNDS = 3
NORM_EPS = 1e-06
PIECE = 8
CHUNKS = 2
VMEM_BYTES = 20 * 1024 * 1024
FULL_VMEM_BYTES = 61 * 1024 * 1024
NT = (((1,), (1,)), ((), ()))


def inverse_length(values):
    return lax.rsqrt(jnp.sum(values * values, axis=-1, keepdims=True) + NORM_EPS)


def halve_kernel(images_ref, texts_ref, half_ref):
    for slot, source in enumerate((images_ref, texts_ref)):
        values = source[...].astype(jnp.float32)
        half_ref[slot] = (values * inverse_length(values)).astype(jnp.bfloat16)


def halve(images, texts):
    rows, width = images.shape
    step = rows // 2
    return pl.pallas_call(
        halve_kernel,
        grid=(rows // step,),
        in_specs=[pl.BlockSpec((step, width), lambda i: (i, 0))] * 2,
        out_specs=pl.BlockSpec((2, step, width), lambda i: (0, i, 0)),
        out_shape=jax.ShapeDtypeStruct((2, rows, width), jnp.bfloat16),
        compiler_params=pltpu.CompilerParams(vmem_limit_bytes=FULL_VMEM_BYTES),
    )(images, texts)


def own_kernel(scalars_ref, half_ref, img_sum_ref, txt_sum_ref, loss_ref):
    scale, bias = scalars_ref[0], scalars_ref[1]
    img, txt = half_ref[0], half_ref[1]
    rows = img.shape[0]
    diagonal = lax.broadcasted_iota(jnp.int32, (rows, rows), 0) == lax.broadcasted_iota(
        jnp.int32, (rows, rows), 1
    )
    logits = scale * lax.dot_general(img, txt, NT, preferred_element_type=jnp.float32) + bias
    signed = jnp.where(diagonal, -logits, logits)
    loss_ref[...] = softplus(signed)
    positive = jnp.where(diagonal, 1.0, 0.0)
    weights = (sigmoid(logits) - positive).astype(jnp.bfloat16)
    img_sum_ref[...] = scale * jnp.dot(weights, txt, preferred_element_type=jnp.float32)
    turned = scale * lax.dot_general(txt, img, NT, preferred_element_type=jnp.float32) + bias
    weights = (sigmoid(turned) - positive).astype(jnp.bfloat16)
    txt_sum_ref[...] = scale * jnp.dot(weights, img, preferred_element_type=jnp.float32)


def softplus(x):
    return jnp.maximum(x, 0.0) + jnp.log1p(jnp.exp(-jnp.abs(x)))


def sigmoid(x):
    return 1.0 / (1.0 + jnp.exp(-x))


def own_terms(scalars, half):
    _, rows, width = half.shape
    return pl.pallas_call(
        own_kernel,
        in_specs=[
            pl.BlockSpec(memory_space=pltpu.SMEM),
            pl.BlockSpec(memory_space=pltpu.VMEM),
        ],
        out_specs=[pl.BlockSpec(memory_space=pltpu.VMEM)] * 3,
        out_shape=[
            jax.ShapeDtypeStruct((rows, width), jnp.float32),
            jax.ShapeDtypeStruct((rows, width), jnp.float32),
            jax.ShapeDtypeStruct((rows, rows), jnp.float32),
        ],
        compiler_params=pltpu.CompilerParams(vmem_limit_bytes=VMEM_BYTES),
        cost_estimate=pl.CostEstimate(
            flops=8 * rows * rows * width, bytes_accessed=12 * rows * width, transcendentals=4 * rows * rows
        ),
    )(scalars, half)


def route_kernel(flips_ref, same_ref, other_ref, out_ref):
    chips = same_ref.shape[0]
    for r in range(ROUNDS):
        chip_flip = flips_ref[r] // 2
        core_flip = flips_ref[r] % 2
        for core, source in enumerate((same_ref, other_ref)):

            @pl.when(core_flip == core)
            def _():
                def copy(t, carry):
                    out_ref[t, r] = source[lax.bitwise_xor(t, chip_flip)]
                    return carry

                lax.fori_loop(0, chips, copy, 0, unroll=8)


def route(flips, same, other):
    chips, piece, width = same.shape
    return pl.pallas_call(
        route_kernel,
        in_specs=[pl.BlockSpec(memory_space=pltpu.SMEM)]
        + [pl.BlockSpec(memory_space=pltpu.VMEM)] * 2,
        out_specs=pl.BlockSpec(memory_space=pltpu.VMEM),
        out_shape=jax.ShapeDtypeStruct((chips, ROUNDS, piece, width), same.dtype),
        compiler_params=pltpu.CompilerParams(vmem_limit_bytes=VMEM_BYTES),
    )(flips, same, other)


def finish(values, summed):
    inverse = inverse_length(values)
    unit = values * inverse
    radial = jnp.sum(unit * summed, axis=-1, keepdims=True)
    return (summed - unit * radial) * inverse


def rounds_kernel(
    scalars_ref, images_ref, texts_ref, half_ref, far_ref, img_sum_ref, txt_sum_ref, own_loss_ref,
    image_grad_ref, text_grad_ref, loss_ref, grads, loss, sems, loss_sem,
):
    scale, bias = scalars_ref[0], scalars_ref[1]
    img, txt = half_ref[0], half_ref[1]
    rows, width = img.shape
    pieces = far_ref.shape[0] // 2
    step = rows // CHUNKS
    copies = []

    def send(slot, source, summed, out_ref):
        for chunk in range(CHUNKS):
            part = pl.ds(chunk * step, step)
            grads[slot, part] = finish(
                source[part].astype(jnp.float32), summed[chunk * step : (chunk + 1) * step]
            )
            copy = pltpu.make_async_copy(grads.at[slot, part], out_ref.at[part], sems.at[slot, chunk])
            copy.start()
            copies.append(copy)

    far_txt = far_ref[pieces:].reshape(ROUNDS * rows, width)
    logits = scale * lax.dot_general(img, far_txt, NT, preferred_element_type=jnp.float32) + bias
    weights = sigmoid(logits).astype(jnp.bfloat16)
    summed = img_sum_ref[...] + scale * jnp.dot(weights, far_txt, preferred_element_type=jnp.float32)
    send(0, images_ref, summed, image_grad_ref)
    parts = softplus(logits)
    losses = own_loss_ref[...]
    for r in range(ROUNDS):
        losses = losses + parts[:, r * rows : (r + 1) * rows]
    loss[...] = jnp.sum(losses.T, axis=0, keepdims=True) * (1.0 / ((ROUNDS + 1) * rows))
    copies.append(pltpu.make_async_copy(loss, loss_ref, loss_sem))
    copies[-1].start()
    summed = txt_sum_ref[...]
    for r in range(ROUNDS):
        far_img = far_ref[:pieces, r].reshape(rows, width)
        logits = scale * lax.dot_general(txt, far_img, NT, preferred_element_type=jnp.float32) + bias
        weights = sigmoid(logits).astype(jnp.bfloat16)
        term = scale * jnp.dot(weights, far_img, preferred_element_type=jnp.float32)
        summed = summed + term.astype(jnp.bfloat16).astype(jnp.float32)
    send(1, texts_ref, summed, text_grad_ref)
    for copy in copies:
        copy.wait()


def all_rounds(scalars, images, texts, half, far, img_sum, txt_sum, losses):
    rows, width = images.shape
    return pl.pallas_call(
        rounds_kernel,
        in_specs=[pl.BlockSpec(memory_space=pltpu.SMEM)]
        + [pl.BlockSpec(memory_space=pltpu.VMEM)] * 7,
        out_specs=[pl.BlockSpec(memory_space=pltpu.HBM)] * 3,
        out_shape=[
            jax.ShapeDtypeStruct((rows, width), jnp.float32),
            jax.ShapeDtypeStruct((rows, width), jnp.float32),
            jax.ShapeDtypeStruct((1, rows), jnp.float32),
        ],
        scratch_shapes=[
            pltpu.VMEM((2, rows, width), jnp.float32),
            pltpu.VMEM((1, rows), jnp.float32),
            pltpu.SemaphoreType.DMA((2, CHUNKS)),
            pltpu.SemaphoreType.DMA,
        ],
        compiler_params=pltpu.CompilerParams(vmem_limit_bytes=VMEM_BYTES),
    )(scalars, images, texts, half, far, img_sum, txt_sum, losses)


def body(num_dev, images, texts, partner, logit_scale, logit_bias):
    rows, width = images.shape
    chips = num_dev // 2
    same_core = [[2 * chip + core for chip in range(chips)] for core in range(2)]
    exchange = functools.partial(
        lax.all_to_all, axis_name="dp", split_axis=0, concat_axis=0, tiled=True, axis_index_groups=same_core
    )
    scalars = jnp.concatenate([logit_scale, logit_bias])
    flips = partner[:, 0]
    half = halve(images, texts)
    spread = exchange(half.reshape(chips, PIECE, width))
    img_sum, txt_sum, losses = own_terms(scalars, half)
    spread, img_sum = lax.optimization_barrier((spread, img_sum))
    sibling = lax.ppermute(spread, "dp", [(i, i ^ 1) for i in range(num_dev)])
    far = exchange(route(flips, spread, sibling))
    image_grad, text_grad, loss = all_rounds(
        scalars, images, texts, half, far, img_sum, txt_sum, losses
    )
    return image_grad, text_grad, loss.reshape(rows)


def solution(mesh):
    return jax.shard_map(
        functools.partial(body, mesh.devices.size),
        mesh=mesh,
        in_specs=(P("dp", None), P("dp", None), P(), P(), P()),
        out_specs=(P("dp", None), P("dp", None), P("dp")),
        check_vma=False,
    )
```

```python
import functools

import jax
import jax.numpy as jnp
from jax import lax
from jax.experimental import pallas as pl
from jax.experimental.pallas import tpu as pltpu
from jax.sharding import PartitionSpec as P

ROUNDS = 3
NORM_EPS = 1e-06
PIECE = 8
CHUNKS = 2
VMEM_BYTES = 20 * 1024 * 1024
FULL_VMEM_BYTES = 60 * 1024 * 1024
NT = (((1,), (1,)), ((), ()))


def inverse_length(values):
    return lax.rsqrt(jnp.sum(values * values, axis=-1, keepdims=True) + NORM_EPS)


def halve_kernel(images_ref, texts_ref, raw_ref, half_ref, sems):
    copies = [
        pltpu.make_async_copy(source, raw_ref.at[slot], sems.at[slot])
        for slot, source in enumerate((images_ref, texts_ref))
    ]
    for copy in copies:
        copy.start()
    for slot, copy in enumerate(copies):
        copy.wait()
        values = raw_ref[slot].astype(jnp.float32)
        half_ref[slot] = (values * inverse_length(values)).astype(jnp.bfloat16)


def halve(images, texts):
    rows, width = images.shape
    return pl.pallas_call(
        halve_kernel,
        in_specs=[pl.BlockSpec(memory_space=pltpu.HBM)] * 2,
        out_specs=[pl.BlockSpec(memory_space=pltpu.VMEM)] * 2,
        out_shape=[pltpu.VMEM((2, rows, width), jnp.bfloat16)] * 2,
        scratch_shapes=[pltpu.SemaphoreType.DMA((2,))],
        compiler_params=pltpu.CompilerParams(vmem_limit_bytes=FULL_VMEM_BYTES),
    )(images, texts)


def own_kernel(scale_ref, bias_ref, half_ref, img_sum_ref, txt_sum_ref, loss_ref):
    scale, bias = scale_ref[0], bias_ref[0]
    img, txt = half_ref[0], half_ref[1]
    rows = img.shape[0]
    diagonal = lax.broadcasted_iota(jnp.int32, (rows, rows), 0) == lax.broadcasted_iota(
        jnp.int32, (rows, rows), 1
    )
    logits = scale * lax.dot_general(img, txt, NT, preferred_element_type=jnp.float32) + bias
    signed = jnp.where(diagonal, -logits, logits)
    loss_ref[...] = softplus(signed)
    positive = jnp.where(diagonal, 1.0, 0.0)
    weights = (sigmoid(logits) - positive).astype(jnp.bfloat16)
    img_sum_ref[...] = scale * jnp.dot(weights, txt, preferred_element_type=jnp.float32)
    turned = scale * lax.dot_general(txt, img, NT, preferred_element_type=jnp.float32) + bias
    weights = (sigmoid(turned) - positive).astype(jnp.bfloat16)
    txt_sum_ref[...] = scale * jnp.dot(weights, img, preferred_element_type=jnp.float32)


def softplus(x):
    return jnp.maximum(x, 0.0) + jnp.log1p(jnp.exp(-jnp.abs(x)))


def sigmoid(x):
    return 1.0 / (1.0 + jnp.exp(-x))


def own_terms(scale, bias, half):
    _, rows, width = half.shape
    return pl.pallas_call(
        own_kernel,
        in_specs=[pl.BlockSpec(memory_space=pltpu.SMEM)] * 2 + [pl.BlockSpec(memory_space=pltpu.VMEM)],
        out_specs=[pl.BlockSpec(memory_space=pltpu.VMEM)] * 3,
        out_shape=[
            jax.ShapeDtypeStruct((rows, width), jnp.float32),
            jax.ShapeDtypeStruct((rows, width), jnp.float32),
            jax.ShapeDtypeStruct((rows, rows), jnp.float32),
        ],
        compiler_params=pltpu.CompilerParams(vmem_limit_bytes=VMEM_BYTES),
        cost_estimate=pl.CostEstimate(
            flops=8 * rows * rows * width, bytes_accessed=12 * rows * width, transcendentals=4 * rows * rows
        ),
    )(scale, bias, half)


def route_kernel(partner_ref, same_ref, other_ref, out_ref):
    chips = same_ref.shape[0]
    for r in range(ROUNDS):
        chip_flip = partner_ref[r, 0] // 2
        core_flip = partner_ref[r, 0] % 2
        for core, source in enumerate((same_ref, other_ref)):

            @pl.when(core_flip == core)
            def _():
                def copy(t, carry):
                    out_ref[t, r] = source[lax.bitwise_xor(t, chip_flip)]
                    return carry

                lax.fori_loop(0, chips, copy, 0, unroll=8)


def route(partner, same, other):
    chips, piece, width = same.shape
    return pl.pallas_call(
        route_kernel,
        in_specs=[pl.BlockSpec(memory_space=pltpu.SMEM)]
        + [pl.BlockSpec(memory_space=pltpu.VMEM)] * 2,
        out_specs=pl.BlockSpec(memory_space=pltpu.VMEM),
        out_shape=jax.ShapeDtypeStruct((chips, ROUNDS, piece, width), same.dtype),
        compiler_params=pltpu.CompilerParams(vmem_limit_bytes=VMEM_BYTES),
    )(partner, same, other)


def finish(values, summed):
    inverse = inverse_length(values)
    unit = values * inverse
    radial = jnp.sum(unit * summed, axis=-1, keepdims=True)
    return (summed - unit * radial) * inverse


def rounds_kernel(
    scale_ref, bias_ref, raw_ref, half_ref, far_ref, img_sum_ref, txt_sum_ref, own_loss_ref,
    image_grad_ref, text_grad_ref, loss_ref, grads, loss, sems, loss_sem,
):
    scale, bias = scale_ref[0], bias_ref[0]
    img, txt = half_ref[0], half_ref[1]
    rows, width = img.shape
    pieces = far_ref.shape[0] // 2
    step = rows // CHUNKS
    copies = []

    def send(slot, summed, out_ref):
        for chunk in range(CHUNKS):
            part = pl.ds(chunk * step, step)
            grads[slot, part] = finish(
                raw_ref[slot, part].astype(jnp.float32), summed[chunk * step : (chunk + 1) * step]
            )
            copy = pltpu.make_async_copy(grads.at[slot, part], out_ref.at[part], sems.at[slot, chunk])
            copy.start()
            copies.append(copy)

    far_txt = far_ref[pieces:].reshape(ROUNDS * rows, width)
    logits = scale * lax.dot_general(img, far_txt, NT, preferred_element_type=jnp.float32) + bias
    weights = sigmoid(logits).astype(jnp.bfloat16)
    summed = img_sum_ref[...] + scale * jnp.dot(weights, far_txt, preferred_element_type=jnp.float32)
    send(0, summed, image_grad_ref)
    parts = softplus(logits)
    losses = own_loss_ref[...]
    for r in range(ROUNDS):
        losses = losses + parts[:, r * rows : (r + 1) * rows]
    loss[...] = jnp.sum(losses.T, axis=0, keepdims=True) * (1.0 / ((ROUNDS + 1) * rows))
    copies.append(pltpu.make_async_copy(loss, loss_ref, loss_sem))
    copies[-1].start()
    summed = txt_sum_ref[...]
    for r in range(ROUNDS):
        far_img = far_ref[:pieces, r].reshape(rows, width)
        logits = scale * lax.dot_general(txt, far_img, NT, preferred_element_type=jnp.float32) + bias
        weights = sigmoid(logits).astype(jnp.bfloat16)
        term = scale * jnp.dot(weights, far_img, preferred_element_type=jnp.float32)
        summed = summed + term.astype(jnp.bfloat16).astype(jnp.float32)
    send(1, summed, text_grad_ref)
    for copy in copies:
        copy.wait()


def all_rounds(scale, bias, raw, half, far, img_sum, txt_sum, losses):
    _, rows, width = raw.shape
    return pl.pallas_call(
        rounds_kernel,
        in_specs=[pl.BlockSpec(memory_space=pltpu.SMEM)] * 2
        + [pl.BlockSpec(memory_space=pltpu.VMEM)] * 6,
        out_specs=[pl.BlockSpec(memory_space=pltpu.HBM)] * 3,
        out_shape=[
            jax.ShapeDtypeStruct((rows, width), jnp.float32),
            jax.ShapeDtypeStruct((rows, width), jnp.float32),
            jax.ShapeDtypeStruct((1, rows), jnp.float32),
        ],
        scratch_shapes=[
            pltpu.VMEM((2, rows, width), jnp.float32),
            pltpu.VMEM((1, rows), jnp.float32),
            pltpu.SemaphoreType.DMA((2, CHUNKS)),
            pltpu.SemaphoreType.DMA,
        ],
        compiler_params=pltpu.CompilerParams(vmem_limit_bytes=VMEM_BYTES),
    )(scale, bias, raw, half, far, img_sum, txt_sum, losses)


def body(num_dev, images, texts, partner, logit_scale, logit_bias):
    rows, width = images.shape
    chips = num_dev // 2
    same_core = [[2 * chip + core for chip in range(chips)] for core in range(2)]
    exchange = functools.partial(
        lax.all_to_all, axis_name="dp", split_axis=0, concat_axis=0, tiled=True, axis_index_groups=same_core
    )
    raw, half = halve(images, texts)
    spread = exchange(half.reshape(chips, PIECE, width))
    half, spread = lax.optimization_barrier((half, spread))
    sibling = lax.ppermute(spread, "dp", [(i, i ^ 1) for i in range(num_dev)])
    img_sum, txt_sum, losses = own_terms(logit_scale, logit_bias, half)
    sibling, img_sum = lax.optimization_barrier((sibling, img_sum))
    far = exchange(route(partner, spread, sibling))
    image_grad, text_grad, loss = all_rounds(
        logit_scale, logit_bias, raw, half, far, img_sum, txt_sum, losses
    )
    return image_grad, text_grad, loss.reshape(rows)


def solution(mesh):
    return jax.shard_map(
        functools.partial(body, mesh.devices.size),
        mesh=mesh,
        in_specs=(P("dp", None), P("dp", None), P(), P(), P()),
        out_specs=(P("dp", None), P("dp", None), P("dp")),
        check_vma=False,
    )
```

```python
import functools

import jax
import jax.numpy as jnp
from jax import lax
from jax.experimental import pallas as pl
from jax.experimental.pallas import tpu as pltpu
from jax.sharding import PartitionSpec as P

ROUNDS = 3
NORM_EPS = 1e-06
PIECE = 8
CHIP_STEPS = (16, 32, 4, 8, 1, 2)
CHUNKS = 2
VMEM_BYTES = 20 * 1024 * 1024
FULL_VMEM_BYTES = 60 * 1024 * 1024
NT = (((1,), (1,)), ((), ()))
TN = (((0,), (0,)), ((), ()))


def inverse_length(values):
    return lax.rsqrt(jnp.sum(values * values, axis=-1, keepdims=True) + NORM_EPS)


def halve_kernel(images_ref, texts_ref, raw_ref, half_ref, inverse_ref, sems):
    copies = [
        pltpu.make_async_copy(source, raw_ref.at[slot], sems.at[slot])
        for slot, source in enumerate((images_ref, texts_ref))
    ]
    for copy in copies:
        copy.start()
    for slot, copy in enumerate(copies):
        copy.wait()
        values = raw_ref[slot].astype(jnp.float32)
        inverse = inverse_length(values)
        inverse_ref[slot] = inverse
        half_ref[slot] = (values * inverse).astype(jnp.bfloat16)


def halve(images, texts):
    rows, width = images.shape
    return pl.pallas_call(
        halve_kernel,
        in_specs=[pl.BlockSpec(memory_space=pltpu.HBM)] * 2,
        out_specs=[pl.BlockSpec(memory_space=pltpu.VMEM)] * 3,
        out_shape=[pltpu.VMEM((2, rows, width), jnp.bfloat16)] * 2 + [pltpu.VMEM((2, rows, 1), jnp.float32)],
        scratch_shapes=[pltpu.SemaphoreType.DMA((2,))],
        compiler_params=pltpu.CompilerParams(vmem_limit_bytes=FULL_VMEM_BYTES),
    )(images, texts)


def own_kernel(scale_ref, bias_ref, half_ref, img_sum_ref, txt_sum_ref, loss_ref):
    scale, bias = scale_ref[0], bias_ref[0]
    img, txt = half_ref[0], half_ref[1]
    rows = img.shape[0]
    diagonal = lax.broadcasted_iota(jnp.int32, (rows, rows), 0) == lax.broadcasted_iota(
        jnp.int32, (rows, rows), 1
    )
    logits = scale * lax.dot_general(img, txt, NT, preferred_element_type=jnp.float32) + bias
    signed = jnp.where(diagonal, -logits, logits)
    loss_ref[...] = softplus(signed)
    positive = jnp.where(diagonal, 1.0, 0.0)
    weights = (sigmoid(logits) - positive).astype(jnp.bfloat16)
    img_sum_ref[...] = scale * jnp.dot(weights, txt, preferred_element_type=jnp.float32)
    txt_sum_ref[...] = scale * lax.dot_general(weights, img, TN, preferred_element_type=jnp.float32)


def softplus(x):
    return jnp.maximum(x, 0.0) + jnp.log1p(jnp.exp(-jnp.abs(x)))


def sigmoid(x):
    return 1.0 / (1.0 + jnp.exp(-x))


def own_terms(scale, bias, half):
    _, rows, width = half.shape
    return pl.pallas_call(
        own_kernel,
        in_specs=[pl.BlockSpec(memory_space=pltpu.SMEM)] * 2 + [pl.BlockSpec(memory_space=pltpu.VMEM)],
        out_specs=[pl.BlockSpec(memory_space=pltpu.VMEM)] * 3,
        out_shape=[
            jax.ShapeDtypeStruct((rows, width), jnp.float32),
            jax.ShapeDtypeStruct((rows, width), jnp.float32),
            jax.ShapeDtypeStruct((rows, rows), jnp.float32),
        ],
        compiler_params=pltpu.CompilerParams(vmem_limit_bytes=VMEM_BYTES),
        cost_estimate=pl.CostEstimate(
            flops=8 * rows * rows * width, bytes_accessed=12 * rows * width, transcendentals=4 * rows * rows
        ),
    )(scale, bias, half)


def slot_chip(slot):
    chip = 0
    for bit, step in enumerate(CHIP_STEPS):
        chip ^= step * ((slot >> bit) & 1)
    return chip


def chip_slot(chip):
    slot = 0
    for bit, step in enumerate(CHIP_STEPS):
        slot += (chip // step % 2) << bit
    return slot


def route_kernel(partner_ref, same_ref, other_ref, out_ref):
    chips = same_ref.shape[0]
    for r in range(ROUNDS):
        chip_flip = chip_slot(partner_ref[r, 0] // 2)
        core_flip = partner_ref[r, 0] % 2
        for core, source in enumerate((same_ref, other_ref)):

            @pl.when(core_flip == core)
            def _():
                def copy(t, carry):
                    out_ref[t, r] = source[lax.bitwise_xor(t, chip_flip)]
                    return carry

                lax.fori_loop(0, chips, copy, 0, unroll=8)


def route(partner, same, other):
    chips, piece, width = same.shape
    return pl.pallas_call(
        route_kernel,
        in_specs=[pl.BlockSpec(memory_space=pltpu.SMEM)]
        + [pl.BlockSpec(memory_space=pltpu.VMEM)] * 2,
        out_specs=pl.BlockSpec(memory_space=pltpu.VMEM),
        out_shape=jax.ShapeDtypeStruct((chips, ROUNDS, piece, width), same.dtype),
        compiler_params=pltpu.CompilerParams(vmem_limit_bytes=VMEM_BYTES),
    )(partner, same, other)


def finish(values, inverse, summed):
    unit = values * inverse
    radial = jnp.sum(unit * summed, axis=-1, keepdims=True)
    return (summed - unit * radial) * inverse


def rounds_kernel(
    scale_ref, bias_ref, raw_ref, half_ref, inverse_ref, far_ref, img_sum_ref, txt_sum_ref, own_loss_ref,
    image_grad_ref, text_grad_ref, loss_ref, grads, loss, sems, loss_sem,
):
    scale, bias = scale_ref[0], bias_ref[0]
    img, txt = half_ref[0], half_ref[1]
    rows, width = img.shape
    pieces = far_ref.shape[0] // 2
    step = rows // CHUNKS
    copies = []

    def send(slot, summed, out_ref):
        for chunk in range(CHUNKS):
            part = pl.ds(chunk * step, step)
            grads[slot, part] = finish(
                raw_ref[slot, part].astype(jnp.float32),
                inverse_ref[slot, part],
                summed[chunk * step : (chunk + 1) * step],
            )
            copy = pltpu.make_async_copy(grads.at[slot, part], out_ref.at[part], sems.at[slot, chunk])
            copy.start()
            copies.append(copy)

    far_txt = far_ref[pieces:].reshape(ROUNDS * rows, width)
    logits = scale * lax.dot_general(img, far_txt, NT, preferred_element_type=jnp.float32) + bias
    weights = sigmoid(logits).astype(jnp.bfloat16)
    summed = img_sum_ref[...] + scale * jnp.dot(weights, far_txt, preferred_element_type=jnp.float32)
    send(0, summed, image_grad_ref)
    parts = softplus(logits)
    losses = own_loss_ref[...]
    for r in range(ROUNDS):
        losses = losses + parts[:, r * rows : (r + 1) * rows]
    loss[...] = jnp.sum(losses.T, axis=0, keepdims=True) * (1.0 / ((ROUNDS + 1) * rows))
    copies.append(pltpu.make_async_copy(loss, loss_ref, loss_sem))
    copies[-1].start()
    summed = txt_sum_ref[...]
    turned = []
    for r in range(ROUNDS):
        far_img = far_ref[:pieces, r].reshape(rows, width)
        logits = scale * lax.dot_general(txt, far_img, NT, preferred_element_type=jnp.float32) + bias
        turned.append(sigmoid(logits).astype(jnp.bfloat16))
    for r in range(ROUNDS):
        far_img = far_ref[:pieces, r].reshape(rows, width)
        weights = turned[r]
        term = scale * jnp.dot(weights, far_img, preferred_element_type=jnp.float32)
        summed = summed + term.astype(jnp.bfloat16).astype(jnp.float32)
    send(1, summed, text_grad_ref)
    for copy in copies:
        copy.wait()


def all_rounds(scale, bias, raw, half, inverse, far, img_sum, txt_sum, losses):
    _, rows, width = raw.shape
    return pl.pallas_call(
        rounds_kernel,
        in_specs=[pl.BlockSpec(memory_space=pltpu.SMEM)] * 2
        + [pl.BlockSpec(memory_space=pltpu.VMEM)] * 7,
        out_specs=[pl.BlockSpec(memory_space=pltpu.HBM)] * 3,
        out_shape=[
            jax.ShapeDtypeStruct((rows, width), jnp.float32),
            jax.ShapeDtypeStruct((rows, width), jnp.float32),
            jax.ShapeDtypeStruct((1, rows), jnp.float32),
        ],
        scratch_shapes=[
            pltpu.VMEM((2, rows, width), jnp.float32),
            pltpu.VMEM((1, rows), jnp.float32),
            pltpu.SemaphoreType.DMA((2, CHUNKS)),
            pltpu.SemaphoreType.DMA,
        ],
        compiler_params=pltpu.CompilerParams(vmem_limit_bytes=VMEM_BYTES),
    )(scale, bias, raw, half, inverse, far, img_sum, txt_sum, losses)


def body(num_dev, images, texts, partner, logit_scale, logit_bias):
    rows, width = images.shape
    chips = num_dev // 2
    same_core = [[2 * slot_chip(slot) + core for slot in range(chips)] for core in range(2)]
    exchange = functools.partial(
        lax.all_to_all, axis_name="dp", split_axis=0, concat_axis=0, tiled=True, axis_index_groups=same_core
    )
    raw, half, inverse = halve(images, texts)
    spread = exchange(half.reshape(chips, PIECE, width))
    half, spread = lax.optimization_barrier((half, spread))
    sibling = lax.ppermute(spread, "dp", [(i, i ^ 1) for i in range(num_dev)])
    img_sum, txt_sum, losses = own_terms(logit_scale, logit_bias, half)
    sibling, img_sum = lax.optimization_barrier((sibling, img_sum))
    far = exchange(route(partner, spread, sibling))
    image_grad, text_grad, loss = all_rounds(
        logit_scale, logit_bias, raw, half, inverse, far, img_sum, txt_sum, losses
    )
    return image_grad, text_grad, loss.reshape(rows)


def solution(mesh):
    return jax.shard_map(
        functools.partial(body, mesh.devices.size),
        mesh=mesh,
        in_specs=(P("dp", None), P("dp", None), P(), P(), P()),
        out_specs=(P("dp", None), P("dp", None), P("dp")),
        check_vma=False,
    )
```

```python
import functools

import jax
import jax.numpy as jnp
from jax import lax
from jax.experimental import pallas as pl
from jax.experimental.pallas import tpu as pltpu
from jax.sharding import PartitionSpec as P

ROUNDS = 3
NORM_EPS = 1e-06
PIECE = 8
CHIP_STEPS = (16, 32, 8, 4, 1, 2)
CHUNKS = 2
VMEM_BYTES = 20 * 1024 * 1024
FULL_VMEM_BYTES = 60 * 1024 * 1024
NT = (((1,), (1,)), ((), ()))
TN = (((0,), (0,)), ((), ()))


def inverse_length(values):
    return lax.rsqrt(jnp.sum(values * values, axis=-1, keepdims=True) + NORM_EPS)


def halve_kernel(images_ref, texts_ref, raw_ref, half_ref, inverse_ref, sems):
    copies = [
        pltpu.make_async_copy(source, raw_ref.at[slot], sems.at[slot])
        for slot, source in enumerate((images_ref, texts_ref))
    ]
    for copy in copies:
        copy.start()
    for slot, copy in enumerate(copies):
        copy.wait()
        values = raw_ref[slot].astype(jnp.float32)
        inverse = inverse_length(values)
        inverse_ref[slot] = inverse
        half_ref[slot] = (values * inverse).astype(jnp.bfloat16)


def halve(images, texts):
    rows, width = images.shape
    return pl.pallas_call(
        halve_kernel,
        in_specs=[pl.BlockSpec(memory_space=pltpu.HBM)] * 2,
        out_specs=[pl.BlockSpec(memory_space=pltpu.VMEM)] * 3,
        out_shape=[pltpu.VMEM((2, rows, width), jnp.bfloat16)] * 2 + [pltpu.VMEM((2, rows, 1), jnp.float32)],
        scratch_shapes=[pltpu.SemaphoreType.DMA((2,))],
        compiler_params=pltpu.CompilerParams(vmem_limit_bytes=FULL_VMEM_BYTES),
    )(images, texts)


def own_kernel(scale_ref, bias_ref, half_ref, img_sum_ref, txt_sum_ref, loss_ref):
    scale, bias = scale_ref[0], bias_ref[0]
    img, txt = half_ref[0], half_ref[1]
    rows = img.shape[0]
    diagonal = lax.broadcasted_iota(jnp.int32, (rows, rows), 0) == lax.broadcasted_iota(
        jnp.int32, (rows, rows), 1
    )
    logits = scale * lax.dot_general(img, txt, NT, preferred_element_type=jnp.float32) + bias
    signed = jnp.where(diagonal, -logits, logits)
    loss_ref[...] = softplus(signed)
    positive = jnp.where(diagonal, 1.0, 0.0)
    weights = (sigmoid(logits) - positive).astype(jnp.bfloat16)
    img_sum_ref[...] = scale * jnp.dot(weights, txt, preferred_element_type=jnp.float32)
    txt_sum_ref[...] = scale * lax.dot_general(weights, img, TN, preferred_element_type=jnp.float32)


def softplus(x):
    return jnp.maximum(x, 0.0) + jnp.log1p(jnp.exp(-jnp.abs(x)))


def sigmoid(x):
    return 1.0 / (1.0 + jnp.exp(-x))


def own_terms(scale, bias, half):
    _, rows, width = half.shape
    return pl.pallas_call(
        own_kernel,
        in_specs=[pl.BlockSpec(memory_space=pltpu.SMEM)] * 2 + [pl.BlockSpec(memory_space=pltpu.VMEM)],
        out_specs=[pl.BlockSpec(memory_space=pltpu.VMEM)] * 3,
        out_shape=[
            jax.ShapeDtypeStruct((rows, width), jnp.float32),
            jax.ShapeDtypeStruct((rows, width), jnp.float32),
            jax.ShapeDtypeStruct((rows, rows), jnp.float32),
        ],
        compiler_params=pltpu.CompilerParams(vmem_limit_bytes=VMEM_BYTES),
        cost_estimate=pl.CostEstimate(
            flops=8 * rows * rows * width, bytes_accessed=12 * rows * width, transcendentals=4 * rows * rows
        ),
    )(scale, bias, half)


def slot_chip(slot):
    chip = 0
    for bit, step in enumerate(CHIP_STEPS):
        chip ^= step * ((slot >> bit) & 1)
    return chip


def chip_slot(chip):
    slot = 0
    for bit, step in enumerate(CHIP_STEPS):
        slot += (chip // step % 2) << bit
    return slot


def route_kernel(partner_ref, same_ref, other_ref, out_ref):
    chips = same_ref.shape[0]
    for r in range(ROUNDS):
        chip_flip = chip_slot(partner_ref[r, 0] // 2)
        core_flip = partner_ref[r, 0] % 2
        for core, source in enumerate((same_ref, other_ref)):

            @pl.when(core_flip == core)
            def _():
                def copy(t, carry):
                    out_ref[t, r] = source[lax.bitwise_xor(t, chip_flip)]
                    return carry

                lax.fori_loop(0, chips, copy, 0, unroll=16)


def route(partner, same, other):
    chips, piece, width = same.shape
    return pl.pallas_call(
        route_kernel,
        in_specs=[pl.BlockSpec(memory_space=pltpu.SMEM)]
        + [pl.BlockSpec(memory_space=pltpu.VMEM)] * 2,
        out_specs=pl.BlockSpec(memory_space=pltpu.VMEM),
        out_shape=jax.ShapeDtypeStruct((chips, ROUNDS, piece, width), same.dtype),
        compiler_params=pltpu.CompilerParams(vmem_limit_bytes=VMEM_BYTES),
    )(partner, same, other)


def finish(values, inverse, summed):
    unit = values * inverse
    radial = jnp.sum(unit * summed, axis=-1, keepdims=True)
    return (summed - unit * radial) * inverse


def rounds_kernel(
    scale_ref, bias_ref, raw_ref, half_ref, inverse_ref, far_ref, img_sum_ref, txt_sum_ref, own_loss_ref,
    image_grad_ref, text_grad_ref, loss_ref, grads, loss, sems, loss_sem,
):
    scale, bias = scale_ref[0], bias_ref[0]
    img, txt = half_ref[0], half_ref[1]
    rows, width = img.shape
    pieces = far_ref.shape[0] // 2
    step = rows // CHUNKS
    copies = []

    def send(slot, summed, out_ref):
        for chunk in range(CHUNKS):
            part = pl.ds(chunk * step, step)
            grads[slot, part] = finish(
                raw_ref[slot, part].astype(jnp.float32),
                inverse_ref[slot, part],
                summed[chunk * step : (chunk + 1) * step],
            )
            copy = pltpu.make_async_copy(grads.at[slot, part], out_ref.at[part], sems.at[slot, chunk])
            copy.start()
            copies.append(copy)

    far_txt = far_ref[pieces:].reshape(ROUNDS * rows, width)
    logits = scale * lax.dot_general(img, far_txt, NT, preferred_element_type=jnp.float32) + bias
    weights = sigmoid(logits).astype(jnp.bfloat16)
    summed = img_sum_ref[...] + scale * jnp.dot(weights, far_txt, preferred_element_type=jnp.float32)
    send(0, summed, image_grad_ref)
    parts = softplus(logits)
    losses = own_loss_ref[...]
    for r in range(ROUNDS):
        losses = losses + parts[:, r * rows : (r + 1) * rows]
    loss[...] = jnp.sum(losses.T, axis=0, keepdims=True) * (1.0 / ((ROUNDS + 1) * rows))
    copies.append(pltpu.make_async_copy(loss, loss_ref, loss_sem))
    copies[-1].start()
    summed = txt_sum_ref[...]
    turned = []
    for r in range(ROUNDS):
        far_img = far_ref[:pieces, r].reshape(rows, width)
        logits = scale * lax.dot_general(txt, far_img, NT, preferred_element_type=jnp.float32) + bias
        turned.append(sigmoid(logits).astype(jnp.bfloat16))
    for r in range(ROUNDS):
        far_img = far_ref[:pieces, r].reshape(rows, width)
        weights = turned[r]
        term = scale * jnp.dot(weights, far_img, preferred_element_type=jnp.float32)
        summed = summed + term.astype(jnp.bfloat16).astype(jnp.float32)
    send(1, summed, text_grad_ref)
    for copy in copies:
        copy.wait()


def all_rounds(scale, bias, raw, half, inverse, far, img_sum, txt_sum, losses):
    _, rows, width = raw.shape
    return pl.pallas_call(
        rounds_kernel,
        in_specs=[pl.BlockSpec(memory_space=pltpu.SMEM)] * 2
        + [pl.BlockSpec(memory_space=pltpu.VMEM)] * 7,
        out_specs=[pl.BlockSpec(memory_space=pltpu.HBM)] * 3,
        out_shape=[
            jax.ShapeDtypeStruct((rows, width), jnp.float32),
            jax.ShapeDtypeStruct((rows, width), jnp.float32),
            jax.ShapeDtypeStruct((1, rows), jnp.float32),
        ],
        scratch_shapes=[
            pltpu.VMEM((2, rows, width), jnp.float32),
            pltpu.VMEM((1, rows), jnp.float32),
            pltpu.SemaphoreType.DMA((2, CHUNKS)),
            pltpu.SemaphoreType.DMA,
        ],
        compiler_params=pltpu.CompilerParams(vmem_limit_bytes=VMEM_BYTES),
    )(scale, bias, raw, half, inverse, far, img_sum, txt_sum, losses)


def body(num_dev, images, texts, partner, logit_scale, logit_bias):
    rows, width = images.shape
    chips = num_dev // 2
    same_core = [[2 * slot_chip(slot) + core for slot in range(chips)] for core in range(2)]
    exchange = functools.partial(
        lax.all_to_all, axis_name="dp", split_axis=0, concat_axis=0, tiled=True, axis_index_groups=same_core
    )
    raw, half, inverse = halve(images, texts)
    spread = exchange(half.reshape(chips, PIECE, width))
    half, spread = lax.optimization_barrier((half, spread))
    sibling = lax.ppermute(spread, "dp", [(i, i ^ 1) for i in range(num_dev)])
    img_sum, txt_sum, losses = own_terms(logit_scale, logit_bias, half)
    sibling, img_sum = lax.optimization_barrier((sibling, img_sum))
    far = exchange(route(partner, spread, sibling))
    image_grad, text_grad, loss = all_rounds(
        logit_scale, logit_bias, raw, half, inverse, far, img_sum, txt_sum, losses
    )
    return image_grad, text_grad, loss.reshape(rows)


def solution(mesh):
    return jax.shard_map(
        functools.partial(body, mesh.devices.size),
        mesh=mesh,
        in_specs=(P("dp", None), P("dp", None), P(), P(), P()),
        out_specs=(P("dp", None), P("dp", None), P("dp")),
        check_vma=False,
    )
```

```python
import functools

import jax
import jax.numpy as jnp
from jax import lax
from jax.experimental import pallas as pl
from jax.experimental.pallas import tpu as pltpu
from jax.sharding import PartitionSpec as P

ROUNDS = 3
NORM_EPS = 1e-06
LOG2_E = 1.4426950408889634
PIECE = 8
CHIP_STEPS = (16, 32, 8, 4, 1, 2)
CHUNKS = 2
VMEM_BYTES = 20 * 1024 * 1024
FULL_VMEM_BYTES = 60 * 1024 * 1024
NT = (((1,), (1,)), ((), ()))
TN = (((0,), (0,)), ((), ()))


def inverse_length(values):
    return lax.rsqrt(jnp.sum(values * values, axis=-1, keepdims=True) + NORM_EPS)


def halve_kernel(images_ref, texts_ref, raw_ref, half_ref, inverse_ref, sems):
    copies = [
        pltpu.make_async_copy(source, raw_ref.at[slot], sems.at[slot])
        for slot, source in enumerate((images_ref, texts_ref))
    ]
    for copy in copies:
        copy.start()
    for slot, copy in enumerate(copies):
        copy.wait()
        values = raw_ref[slot].astype(jnp.float32)
        inverse = inverse_length(values)
        inverse_ref[slot] = inverse
        half_ref[slot] = (values * inverse).astype(jnp.bfloat16)


def halve(images, texts):
    rows, width = images.shape
    return pl.pallas_call(
        halve_kernel,
        in_specs=[pl.BlockSpec(memory_space=pltpu.HBM)] * 2,
        out_specs=[pl.BlockSpec(memory_space=pltpu.VMEM)] * 3,
        out_shape=[pltpu.VMEM((2, rows, width), jnp.bfloat16)] * 2 + [pltpu.VMEM((2, rows, 1), jnp.float32)],
        scratch_shapes=[pltpu.SemaphoreType.DMA((2,))],
        compiler_params=pltpu.CompilerParams(vmem_limit_bytes=FULL_VMEM_BYTES),
    )(images, texts)


def own_kernel(scale_ref, bias_ref, half_ref, img_sum_ref, txt_sum_ref, loss_ref):
    scale, bias = scale_ref[0], bias_ref[0]
    img, txt = half_ref[0], half_ref[1]
    rows = img.shape[0]
    diagonal = lax.broadcasted_iota(jnp.int32, (rows, rows), 0) == lax.broadcasted_iota(
        jnp.int32, (rows, rows), 1
    )
    logits = scale * lax.dot_general(img, txt, NT, preferred_element_type=jnp.float32) + bias
    signed = jnp.where(diagonal, -logits, logits)
    loss_ref[...] = softplus(signed)
    positive = jnp.where(diagonal, 1.0, 0.0)
    weights = (sigmoid(logits) - positive).astype(jnp.bfloat16)
    img_sum_ref[...] = scale * jnp.dot(weights, txt, preferred_element_type=jnp.float32)
    txt_sum_ref[...] = scale * lax.dot_general(weights, img, TN, preferred_element_type=jnp.float32)


def softplus(x):
    return jnp.maximum(x, 0.0) + jnp.log1p(jnp.exp(-jnp.abs(x)))


def sigmoid(x):
    return 1.0 / (1.0 + jnp.exp(-x))


def own_terms(scale, bias, half):
    _, rows, width = half.shape
    return pl.pallas_call(
        own_kernel,
        in_specs=[pl.BlockSpec(memory_space=pltpu.SMEM)] * 2 + [pl.BlockSpec(memory_space=pltpu.VMEM)],
        out_specs=[pl.BlockSpec(memory_space=pltpu.VMEM)] * 3,
        out_shape=[
            jax.ShapeDtypeStruct((rows, width), jnp.float32),
            jax.ShapeDtypeStruct((rows, width), jnp.float32),
            jax.ShapeDtypeStruct((rows, rows), jnp.float32),
        ],
        compiler_params=pltpu.CompilerParams(vmem_limit_bytes=VMEM_BYTES),
        cost_estimate=pl.CostEstimate(
            flops=8 * rows * rows * width, bytes_accessed=12 * rows * width, transcendentals=4 * rows * rows
        ),
    )(scale, bias, half)


def slot_chip(slot):
    chip = 0
    for bit, step in enumerate(CHIP_STEPS):
        chip ^= step * ((slot >> bit) & 1)
    return chip


def chip_slot(chip):
    slot = 0
    for bit, step in enumerate(CHIP_STEPS):
        slot += (chip // step % 2) << bit
    return slot


def route_kernel(partner_ref, same_ref, other_ref, out_ref):
    chips = same_ref.shape[0]
    for r in range(ROUNDS):
        chip_flip = chip_slot(partner_ref[r, 0] // 2)
        core_flip = partner_ref[r, 0] % 2
        for core, source in enumerate((same_ref, other_ref)):

            @pl.when(core_flip == core)
            def _():
                def copy(t, carry):
                    out_ref[t, r] = source[lax.bitwise_xor(t, chip_flip)]
                    return carry

                lax.fori_loop(0, chips, copy, 0, unroll=16)


def route(partner, same, other):
    chips, piece, width = same.shape
    return pl.pallas_call(
        route_kernel,
        in_specs=[pl.BlockSpec(memory_space=pltpu.SMEM)]
        + [pl.BlockSpec(memory_space=pltpu.VMEM)] * 2,
        out_specs=pl.BlockSpec(memory_space=pltpu.VMEM),
        out_shape=jax.ShapeDtypeStruct((chips, ROUNDS, piece, width), same.dtype),
        compiler_params=pltpu.CompilerParams(vmem_limit_bytes=VMEM_BYTES),
    )(partner, same, other)


def finish(values, inverse, summed):
    unit = values * inverse
    radial = jnp.sum(unit * summed, axis=-1, keepdims=True)
    return (summed - unit * radial) * inverse


def rounds_kernel(
    scale_ref, bias_ref, raw_ref, half_ref, inverse_ref, far_ref, img_sum_ref, txt_sum_ref, own_loss_ref,
    image_grad_ref, text_grad_ref, loss_ref, grads, loss, sems, loss_sem,
):
    scale, bias = scale_ref[0], bias_ref[0]
    img, txt = half_ref[0], half_ref[1]
    rows, width = img.shape
    pieces = far_ref.shape[0] // 2
    step = rows // CHUNKS
    copies = []

    def send(slot, summed, out_ref):
        for chunk in range(CHUNKS):
            part = pl.ds(chunk * step, step)
            grads[slot, part] = finish(
                raw_ref[slot, part].astype(jnp.float32),
                inverse_ref[slot, part],
                summed[chunk * step : (chunk + 1) * step],
            )
            copy = pltpu.make_async_copy(grads.at[slot, part], out_ref.at[part], sems.at[slot, chunk])
            copy.start()
            copies.append(copy)

    far_txt = far_ref[pieces:].reshape(ROUNDS * rows, width)
    logits = scale * lax.dot_general(img, far_txt, NT, preferred_element_type=jnp.float32) + bias
    weights = sigmoid(logits).astype(jnp.bfloat16)
    summed = img_sum_ref[...] + scale * jnp.dot(weights, far_txt, preferred_element_type=jnp.float32)
    send(0, summed, image_grad_ref)
    parts = softplus(logits)
    losses = own_loss_ref[...]
    for r in range(ROUNDS):
        losses = losses + parts[:, r * rows : (r + 1) * rows]
    loss[...] = jnp.sum(losses.T, axis=0, keepdims=True) * (1.0 / ((ROUNDS + 1) * rows))
    copies.append(pltpu.make_async_copy(loss, loss_ref, loss_sem))
    copies[-1].start()
    summed = txt_sum_ref[...]
    steep, shift = -LOG2_E * scale, -LOG2_E * bias
    turned = []
    for r in range(ROUNDS):
        far_img = far_ref[:pieces, r].reshape(rows, width)
        product = lax.dot_general(txt, far_img, NT, preferred_element_type=jnp.float32)
        turned.append((1.0 / (1.0 + jnp.exp2(steep * product + shift))).astype(jnp.bfloat16))
    for r in range(ROUNDS):
        far_img = far_ref[:pieces, r].reshape(rows, width)
        weights = turned[r]
        term = scale * jnp.dot(weights, far_img, preferred_element_type=jnp.float32)
        summed = summed + term.astype(jnp.bfloat16).astype(jnp.float32)
    send(1, summed, text_grad_ref)
    for copy in copies:
        copy.wait()


def all_rounds(scale, bias, raw, half, inverse, far, img_sum, txt_sum, losses):
    _, rows, width = raw.shape
    return pl.pallas_call(
        rounds_kernel,
        in_specs=[pl.BlockSpec(memory_space=pltpu.SMEM)] * 2
        + [pl.BlockSpec(memory_space=pltpu.VMEM)] * 7,
        out_specs=[pl.BlockSpec(memory_space=pltpu.HBM)] * 3,
        out_shape=[
            jax.ShapeDtypeStruct((rows, width), jnp.float32),
            jax.ShapeDtypeStruct((rows, width), jnp.float32),
            jax.ShapeDtypeStruct((1, rows), jnp.float32),
        ],
        scratch_shapes=[
            pltpu.VMEM((2, rows, width), jnp.float32),
            pltpu.VMEM((1, rows), jnp.float32),
            pltpu.SemaphoreType.DMA((2, CHUNKS)),
            pltpu.SemaphoreType.DMA,
        ],
        compiler_params=pltpu.CompilerParams(vmem_limit_bytes=VMEM_BYTES),
    )(scale, bias, raw, half, inverse, far, img_sum, txt_sum, losses)


def body(num_dev, images, texts, partner, logit_scale, logit_bias):
    rows, width = images.shape
    chips = num_dev // 2
    same_core = [[2 * slot_chip(slot) + core for slot in range(chips)] for core in range(2)]
    exchange = functools.partial(
        lax.all_to_all, axis_name="dp", split_axis=0, concat_axis=0, tiled=True, axis_index_groups=same_core
    )
    raw, half, inverse = halve(images, texts)
    spread = exchange(half.reshape(chips, PIECE, width))
    half, spread = lax.optimization_barrier((half, spread))
    sibling = lax.ppermute(spread, "dp", [(i, i ^ 1) for i in range(num_dev)])
    img_sum, txt_sum, losses = own_terms(logit_scale, logit_bias, half)
    sibling, img_sum = lax.optimization_barrier((sibling, img_sum))
    far = exchange(route(partner, spread, sibling))
    image_grad, text_grad, loss = all_rounds(
        logit_scale, logit_bias, raw, half, inverse, far, img_sum, txt_sum, losses
    )
    return image_grad, text_grad, loss.reshape(rows)


def solution(mesh):
    return jax.shard_map(
        functools.partial(body, mesh.devices.size),
        mesh=mesh,
        in_specs=(P("dp", None), P("dp", None), P(), P(), P()),
        out_specs=(P("dp", None), P("dp", None), P("dp")),
        check_vma=False,
    )
```

```python
import functools

import jax
import jax.numpy as jnp
from jax import lax
from jax.experimental import pallas as pl
from jax.experimental.pallas import tpu as pltpu
from jax.sharding import PartitionSpec as P

ROUNDS = 3
NORM_EPS = 1e-06
LOG2_E = 1.4426950408889634
PIECE = 8
CHIP_STEPS = (16, 32, 8, 4, 1, 2)
CHUNKS = 2
VMEM_BYTES = 20 * 1024 * 1024
FULL_VMEM_BYTES = 60 * 1024 * 1024
NT = (((1,), (1,)), ((), ()))
TN = (((0,), (0,)), ((), ()))


def inverse_length(values):
    return lax.rsqrt(jnp.sum(values * values, axis=-1, keepdims=True) + NORM_EPS)


def halve_kernel(images_ref, texts_ref, raw_ref, half_ref, inverse_ref, sems):
    copies = [
        pltpu.make_async_copy(source, raw_ref.at[slot], sems.at[slot])
        for slot, source in enumerate((images_ref, texts_ref))
    ]
    for copy in copies:
        copy.start()
    for slot, copy in enumerate(copies):
        copy.wait()
        values = raw_ref[slot].astype(jnp.float32)
        inverse = inverse_length(values)
        inverse_ref[slot] = inverse
        half_ref[slot] = (values * inverse).astype(jnp.bfloat16)


def halve(images, texts):
    rows, width = images.shape
    return pl.pallas_call(
        halve_kernel,
        in_specs=[pl.BlockSpec(memory_space=pltpu.HBM)] * 2,
        out_specs=[pl.BlockSpec(memory_space=pltpu.VMEM)] * 3,
        out_shape=[pltpu.VMEM((2, rows, width), jnp.bfloat16)] * 2 + [pltpu.VMEM((2, rows, 1), jnp.float32)],
        scratch_shapes=[pltpu.SemaphoreType.DMA((2,))],
        compiler_params=pltpu.CompilerParams(vmem_limit_bytes=FULL_VMEM_BYTES),
    )(images, texts)


def own_kernel(scale_ref, bias_ref, half_ref, img_sum_ref, txt_sum_ref, loss_ref):
    scale, bias = scale_ref[0], bias_ref[0]
    img, txt = half_ref[0], half_ref[1]
    rows = img.shape[0]
    diagonal = lax.broadcasted_iota(jnp.int32, (rows, rows), 0) == lax.broadcasted_iota(
        jnp.int32, (rows, rows), 1
    )
    logits = scale * lax.dot_general(img, txt, NT, preferred_element_type=jnp.float32) + bias
    signed = jnp.where(diagonal, -logits, logits)
    loss_ref[...] = softplus(signed)
    positive = jnp.where(diagonal, 1.0, 0.0)
    weights = (sigmoid(logits) - positive).astype(jnp.bfloat16)
    img_sum_ref[...] = scale * jnp.dot(weights, txt, preferred_element_type=jnp.float32)
    txt_sum_ref[...] = scale * lax.dot_general(weights, img, TN, preferred_element_type=jnp.float32)


def softplus(x):
    return jnp.maximum(x, 0.0) + jnp.log1p(jnp.exp(-jnp.abs(x)))


def sigmoid(x):
    return 1.0 / (1.0 + jnp.exp(-x))


def own_terms(scale, bias, half):
    _, rows, width = half.shape
    return pl.pallas_call(
        own_kernel,
        in_specs=[pl.BlockSpec(memory_space=pltpu.SMEM)] * 2 + [pl.BlockSpec(memory_space=pltpu.VMEM)],
        out_specs=[pl.BlockSpec(memory_space=pltpu.VMEM)] * 3,
        out_shape=[
            jax.ShapeDtypeStruct((rows, width), jnp.float32),
            jax.ShapeDtypeStruct((rows, width), jnp.float32),
            jax.ShapeDtypeStruct((rows, rows), jnp.float32),
        ],
        compiler_params=pltpu.CompilerParams(vmem_limit_bytes=VMEM_BYTES),
        cost_estimate=pl.CostEstimate(
            flops=8 * rows * rows * width, bytes_accessed=12 * rows * width, transcendentals=4 * rows * rows
        ),
    )(scale, bias, half)


def slot_chip(slot):
    chip = 0
    for bit, step in enumerate(CHIP_STEPS):
        chip ^= step * ((slot >> bit) & 1)
    return chip


def chip_slot(chip):
    slot = 0
    for bit, step in enumerate(CHIP_STEPS):
        slot += (chip // step % 2) << bit
    return slot


def route_kernel(partner_ref, same_ref, other_ref, out_ref):
    chips = same_ref.shape[0]
    for r in range(ROUNDS):
        chip_flip = chip_slot(partner_ref[r, 0] // 2)
        core_flip = partner_ref[r, 0] % 2
        for core, source in enumerate((same_ref, other_ref)):

            @pl.when(core_flip == core)
            def _():
                def copy(t, carry):
                    out_ref[t, r] = source[lax.bitwise_xor(t, chip_flip)]
                    return carry

                lax.fori_loop(0, chips, copy, 0, unroll=32)


def route(partner, same, other):
    chips, piece, width = same.shape
    return pl.pallas_call(
        route_kernel,
        in_specs=[pl.BlockSpec(memory_space=pltpu.SMEM)]
        + [pl.BlockSpec(memory_space=pltpu.VMEM)] * 2,
        out_specs=pl.BlockSpec(memory_space=pltpu.VMEM),
        out_shape=jax.ShapeDtypeStruct((chips, ROUNDS, piece, width), same.dtype),
        compiler_params=pltpu.CompilerParams(vmem_limit_bytes=VMEM_BYTES),
    )(partner, same, other)


def finish(values, inverse, summed):
    unit = values * inverse
    radial = jnp.sum(unit * summed, axis=-1, keepdims=True)
    return (summed - unit * radial) * inverse


def rounds_kernel(
    scale_ref, bias_ref, raw_ref, half_ref, inverse_ref, far_ref, img_sum_ref, txt_sum_ref, own_loss_ref,
    image_grad_ref, text_grad_ref, loss_ref, grads, loss, sems, loss_sem,
):
    scale, bias = scale_ref[0], bias_ref[0]
    img, txt = half_ref[0], half_ref[1]
    rows, width = img.shape
    pieces = far_ref.shape[0] // 2
    step = rows // CHUNKS
    copies = []

    def send(slot, summed, out_ref):
        for chunk in range(CHUNKS):
            part = pl.ds(chunk * step, step)
            grads[slot, part] = finish(
                raw_ref[slot, part].astype(jnp.float32),
                inverse_ref[slot, part],
                summed[chunk * step : (chunk + 1) * step],
            )
            copy = pltpu.make_async_copy(grads.at[slot, part], out_ref.at[part], sems.at[slot, chunk])
            copy.start()
            copies.append(copy)

    far_txt = far_ref[pieces:].reshape(ROUNDS * rows, width)
    logits = scale * lax.dot_general(img, far_txt, NT, preferred_element_type=jnp.float32) + bias
    weights = sigmoid(logits).astype(jnp.bfloat16)
    summed = img_sum_ref[...] + scale * jnp.dot(weights, far_txt, preferred_element_type=jnp.float32)
    send(0, summed, image_grad_ref)
    parts = softplus(logits)
    losses = own_loss_ref[...]
    for r in range(ROUNDS):
        losses = losses + parts[:, r * rows : (r + 1) * rows]
    loss[...] = jnp.sum(losses.T, axis=0, keepdims=True) * (1.0 / ((ROUNDS + 1) * rows))
    copies.append(pltpu.make_async_copy(loss, loss_ref, loss_sem))
    copies[-1].start()
    summed = txt_sum_ref[...]
    steep, shift = -LOG2_E * scale, -LOG2_E * bias
    turned = []
    for r in range(ROUNDS):
        far_img = far_ref[:pieces, r].reshape(rows, width)
        product = lax.dot_general(txt, far_img, NT, preferred_element_type=jnp.float32)
        turned.append((1.0 / (1.0 + jnp.exp2(steep * product + shift))).astype(jnp.bfloat16))
    for r in range(ROUNDS):
        far_img = far_ref[:pieces, r].reshape(rows, width)
        weights = turned[r]
        term = scale * jnp.dot(weights, far_img, preferred_element_type=jnp.float32)
        summed = summed + term.astype(jnp.bfloat16).astype(jnp.float32)
    send(1, summed, text_grad_ref)
    for copy in copies:
        copy.wait()


def all_rounds(scale, bias, raw, half, inverse, far, img_sum, txt_sum, losses):
    _, rows, width = raw.shape
    return pl.pallas_call(
        rounds_kernel,
        in_specs=[pl.BlockSpec(memory_space=pltpu.SMEM)] * 2
        + [pl.BlockSpec(memory_space=pltpu.VMEM)] * 7,
        out_specs=[pl.BlockSpec(memory_space=pltpu.HBM)] * 3,
        out_shape=[
            jax.ShapeDtypeStruct((rows, width), jnp.float32),
            jax.ShapeDtypeStruct((rows, width), jnp.float32),
            jax.ShapeDtypeStruct((1, rows), jnp.float32),
        ],
        scratch_shapes=[
            pltpu.VMEM((2, rows, width), jnp.float32),
            pltpu.VMEM((1, rows), jnp.float32),
            pltpu.SemaphoreType.DMA((2, CHUNKS)),
            pltpu.SemaphoreType.DMA,
        ],
        compiler_params=pltpu.CompilerParams(vmem_limit_bytes=VMEM_BYTES),
    )(scale, bias, raw, half, inverse, far, img_sum, txt_sum, losses)


def body(num_dev, images, texts, partner, logit_scale, logit_bias):
    rows, width = images.shape
    chips = num_dev // 2
    same_core = [[2 * slot_chip(slot) + core for slot in range(chips)] for core in range(2)]
    exchange = functools.partial(
        lax.all_to_all, axis_name="dp", split_axis=0, concat_axis=0, tiled=True, axis_index_groups=same_core
    )
    raw, half, inverse = halve(images, texts)
    spread = exchange(half.reshape(chips, PIECE, width))
    half, spread = lax.optimization_barrier((half, spread))
    sibling = lax.ppermute(spread, "dp", [(i, i ^ 1) for i in range(num_dev)])
    img_sum, txt_sum, losses = own_terms(logit_scale, logit_bias, half)
    sibling, img_sum = lax.optimization_barrier((sibling, img_sum))
    far = exchange(route(partner, spread, sibling))
    image_grad, text_grad, loss = all_rounds(
        logit_scale, logit_bias, raw, half, inverse, far, img_sum, txt_sum, losses
    )
    return image_grad, text_grad, loss.reshape(rows)


def solution(mesh):
    return jax.shard_map(
        functools.partial(body, mesh.devices.size),
        mesh=mesh,
        in_specs=(P("dp", None), P("dp", None), P(), P(), P()),
        out_specs=(P("dp", None), P("dp", None), P("dp")),
        check_vma=False,
    )
```
